128 devices in a mesh: fsdp: 8 (over z_lo, y), bulk: 16 (over x, z_hi, core).
Axes of the slice: x: 4, y: 4, z: 4 (z_hi: 2, z_lo: 2; z = z_hi * 2 + z_lo), core: 2. Of those that a mesh axis runs over, the one named last changes fastest.
Arguments:
- q_nope: bfloat16 [1536, 8192], P(('fsdp', 'bulk')), may hold values from -0.5 to 0.5
- kv_up: bfloat16 [512, 16384], P(('fsdp', 'bulk')), may hold values from -6 to 6
- o_proj: bfloat16 [8192, 7168], P(('fsdp', 'bulk')), may hold values from -0.5 to 0.5
Outputs:
- q_absorbed: bfloat16 [64, 1536, 512], P('fsdp')
- out_absorbed: bfloat16 [64, 512, 7168], P('fsdp', None, 'bulk')
The draws below stay inside these ranges and needn't reach their ends.
All inputs are finite; a program needn't handle non-finite values.
Results may differ from the reference program's by a relative error of at most 0.001.
Values may be sent and summed in bfloat16 or wider, within the bound.
No kernel may reach another device: no remote copies, remote signals or barrier semaphores. Data moves between devices by JAX's collectives and lax.ppermute only.
A program may use at most 128 MiB of HBM per device.

```python
import jax
import jax.numpy as jnp
from jax import lax

H = 64
QL = 1536
KVL = 512
NOPE = 128
VD = 128
D = 7168


def block_levels(own_key, extent, cuts, smallest, top_value):
    factor_of = 1.0
    for axis_at, shards_of in cuts:
        heights = jax.random.uniform(jax.random.fold_in(jax.random.fold_in(own_key, 6), axis_at), (shards_of,), jnp.float32, smallest / len(cuts), top_value / len(cuts))
        factor_of = factor_of * jnp.repeat(jnp.exp(heights), extent[axis_at] // shards_of).reshape((-1,) + (1,) * (len(extent) - 1 - axis_at))
    return factor_of


def noise(own_key, extent, scale, most, cuts=(), dtype=jnp.bfloat16):
    factor_of = block_levels(own_key, extent, cuts, -0.22, 0.18) if cuts else 1.0
    array = jax.random.normal(own_key, extent, jnp.float32) * scale * factor_of
    return jnp.minimum(jnp.maximum(array, -most), most).astype(dtype)


def setup_inputs(seed: int = 0) -> dict:
    key_of = jax.random.split(jax.random.key(seed), 4)
    q_nope = noise(key_of[0], (QL, H * NOPE), NOPE ** -0.5, 0.5, ((0, 128),))
    kv_up = noise(key_of[1], (KVL, H * (NOPE + VD)), 1.0, 6.0, ((0, 128),))
    o_proj = noise(key_of[2], (H * VD, D), VD ** -0.5, 0.5, ((0, 128),))
    return dict(q_nope=q_nope, kv_up=kv_up, o_proj=o_proj)


def reference(q_nope, kv_up, o_proj):
    query_heads = q_nope.reshape(QL, H, NOPE).transpose(1, 0, 2)
    latent_heads = kv_up.reshape(KVL, H, NOPE + VD).transpose(1, 0, 2)
    output_heads = o_proj.reshape(H, VD, D)

    def one_head(pieces):
        query_one, latent_one, output_one = pieces
        key_one = latent_one[:, :NOPE]
        value_one = latent_one[:, NOPE:]
        query_block = jnp.dot(query_one, key_one.T, preferred_element_type=jnp.float32).astype(jnp.bfloat16)
        output_block = jnp.dot(value_one, output_one, preferred_element_type=jnp.float32).astype(jnp.bfloat16)
        return query_block, output_block

    q_absorbed, out_absorbed = lax.map(one_head, (query_heads, latent_heads, output_heads))
    return q_absorbed, out_absorbed
```

```python
import jax
import jax.numpy as jnp
from jax import lax
from jax.sharding import PartitionSpec as P

QL = 1536
KVL = 512
NOPE = 128
VD = 128


def on_device(q_nope, kv_up, o_proj):
    n_fsdp = lax.axis_size("fsdp")
    q_rows, q_cols = q_nope.shape
    kv_rows, kv_cols = kv_up.shape
    n_bulk = lax.axis_size("bulk")
    own_cols = q_cols // n_fsdp
    heads = own_cols // NOPE
    q_send = q_nope.reshape(q_rows, n_fsdp, own_cols).transpose(1, 0, 2)
    kv_send = kv_up.reshape(kv_rows, n_fsdp, kv_cols // n_fsdp).transpose(1, 0, 2)
    kv_part = lax.all_to_all(kv_send, "fsdp", split_axis=0, concat_axis=0, tiled=True)
    q_part = lax.all_to_all(q_send, "fsdp", split_axis=0, concat_axis=0, tiled=True)
    kv_all = lax.all_gather(kv_part.reshape(n_fsdp * kv_rows, -1), "bulk", axis=0)
    q_all = lax.all_gather(q_part.reshape(n_fsdp * q_rows, -1), "bulk", axis=0)
    output_rows = lax.all_to_all(o_proj, "bulk", split_axis=1, concat_axis=0, tiled=True)
    latent = kv_all.reshape(n_bulk, n_fsdp, kv_rows, -1).transpose(1, 0, 2, 3)
    latent = latent.reshape(KVL, heads, NOPE + VD)
    query = q_all.reshape(n_bulk, n_fsdp, q_rows, -1).transpose(1, 0, 2, 3)
    query = query.reshape(QL, heads, NOPE)
    q_absorbed = jnp.einsum(
        "rhn,lhn->hrl", query, latent[:, :, :NOPE], preferred_element_type=jnp.float32
    ).astype(jnp.bfloat16)
    output_heads = output_rows.reshape(heads, VD, output_rows.shape[1])
    out_absorbed = jnp.einsum(
        "lhv,hvd->hld", latent[:, :, NOPE:], output_heads, preferred_element_type=jnp.float32
    ).astype(jnp.bfloat16)
    return (q_absorbed, out_absorbed)


def solution(mesh):
    in_specs = (P(("fsdp", "bulk"), None), P(("fsdp", "bulk"), None), P(("fsdp", "bulk"), None))
    out_specs = (P("fsdp", None, None), P("fsdp", None, "bulk"))
    return jax.shard_map(
        on_device, mesh=mesh, in_specs=in_specs, out_specs=out_specs, check_vma=False
    )
```

```python
import functools

import jax
import jax.numpy as jnp
import numpy as np
from jax import lax
from jax.experimental import pallas as pl
from jax.experimental.pallas import tpu as pltpu
from jax.sharding import Mesh, PartitionSpec as P

QL = 1536
KVL = 512
NOPE = 128
VD = 128
X, ZH, ZL, Y, C = 4, 2, 2, 4, 2
BULK = ("x", "zh", "c")
F = ZL * Y
HALF = 4
Q_BLOCK = ZH * C * 12
L_BLOCK = ZH * C * 4
MSG_ROWS = Q_BLOCK + 2 * L_BLOCK
D_PART = 448


def shifts(dx, dz, dc):
    at = lambda x, z, c: (x * ZH + z) * C + c
    return [
        (at(x, z, c), at((x + dx) % X, (z + dz) % ZH, (c + dc) % C))
        for x in range(X)
        for z in range(ZH)
        for c in range(C)
    ]


def absorb_kernel(s_ref, *refs):
    m_refs, o_refs, rest = refs[:4], refs[4:8], refs[8:]
    q_out, d_out, kv = rest[-3:]
    i = pl.program_id(0)
    x, zh, c, base = s_ref[0], s_ref[1], s_ref[2], s_ref[3]
    q_cols = pl.ds(pl.multiple_of(i * NOPE, NOPE), NOPE)
    kv_cols = pl.ds(pl.multiple_of((i % 2) * 256, 256), 256)
    kv_rows = pl.ds(pl.multiple_of(Q_BLOCK + (i // 2) * L_BLOCK, L_BLOCK), L_BLOCK)
    for d in range(X):
        xs = lax.rem(x - d + X, X)
        for f in range(F):
            at = pl.multiple_of(f * (X * L_BLOCK) + xs * L_BLOCK, L_BLOCK)
            kv[pl.ds(at, L_BLOCK), :] = m_refs[d][f, kv_rows, kv_cols]
    key = kv[:, :NOPE]
    for d in range(X):
        xs = lax.rem(x - d + X, X)
        query = m_refs[d][:, :Q_BLOCK, q_cols].reshape(F * Q_BLOCK, NOPE)
        block = lax.dot_general(
            query, key, (((1,), (1,)), ((), ())), preferred_element_type=jnp.float32
        ).astype(jnp.bfloat16)
        for f in range(F):
            at = pl.multiple_of(f * (X * Q_BLOCK) + xs * Q_BLOCK, 16)
            q_out[0, pl.ds(at, Q_BLOCK), :] = block[f * Q_BLOCK : (f + 1) * Q_BLOCK]
    value = kv[:, NOPE:]
    head = base + i
    same_z = (head % ZH) == zh
    for core in range(C):

        @pl.when(c == core)
        def _():
            cols = slice(core * 384, core * 384 + 512)
            own = jnp.where(same_z, o_refs[0][0, :, cols], o_refs[1][0, :, cols])
            other = jnp.where(same_z, o_refs[2][0, :, cols], o_refs[3][0, :, cols])
            rows = (own, other) if core == 0 else (other, own)
            out_head = jnp.concatenate(rows, axis=0)
            block = lax.dot_general(
                out_head, value, (((0,), (1,)), ((), ())), preferred_element_type=jnp.float32
            ).astype(jnp.bfloat16)
            d_out[0] = block[core * 64 : core * 64 + D_PART]


def absorb(scalars, messages, o_parts, earlier=None):
    def o_index(i, s):
        return (lax.rem(s[0] - (s[3] + i) // ZH + X, X), 0, 0)

    whole = pl.BlockSpec((F, MSG_ROWS, HALF * NOPE), lambda i, s: (0, 0, 0))
    o_spec = pl.BlockSpec((1, 64, 2 * D_PART), o_index)
    in_specs = [whole] * 4 + [o_spec] * 4
    operands = [*messages, *o_parts]
    aliases = {}
    if earlier is not None:
        in_specs += [pl.BlockSpec(memory_space=pl.ANY)] * 2
        operands += list(earlier)
        aliases = {9: 0, 10: 1}
    return pl.pallas_call(
        absorb_kernel,
        grid_spec=pltpu.PrefetchScalarGridSpec(
            num_scalar_prefetch=1,
            grid=(HALF,),
            in_specs=in_specs,
            out_specs=[
                pl.BlockSpec((1, QL, KVL), lambda i, s: (s[3] + i, 0, 0)),
                pl.BlockSpec((1, D_PART, KVL), lambda i, s: (s[3] + i, 0, 0)),
            ],
            scratch_shapes=[pltpu.VMEM((KVL, NOPE + VD), jnp.bfloat16)],
        ),
        out_shape=[
            jax.ShapeDtypeStruct((2 * HALF, QL, KVL), jnp.bfloat16),
            jax.ShapeDtypeStruct((2 * HALF, D_PART, KVL), jnp.bfloat16),
        ],
        input_output_aliases=aliases,
        compiler_params=pltpu.CompilerParams(vmem_limit_bytes=24 * 2**20),
        cost_estimate=pl.CostEstimate(
            flops=2 * HALF * NOPE * KVL * (QL + 512),
            bytes_accessed=HALF * 2 * KVL * (QL + D_PART) + 4 * 655360,
            transcendentals=0,
        ),
    )(scalars, *operands)


def on_device(q_nope, kv_up, o_proj):
    x, zh, c = lax.axis_index("x"), lax.axis_index("zh"), lax.axis_index("c")
    over = lambda a, *d: lax.ppermute(a, BULK, shifts(*d))

    o_cols = o_proj.shape[1] // X
    o_of = lambda d: lax.dynamic_slice_in_dim(o_proj, lax.rem(x + d, X) * o_cols, o_cols, 1)
    o_x = {d: over(o_of(d), d, 0, 0) for d in (2, 1, 3)}
    o_x[0] = o_of(0)

    q = q_nope.reshape(3, 4, F * C, HALF * NOPE).transpose(2, 0, 1, 3)
    kv = kv_up.reshape(4, F * C, 2, HALF * NOPE).transpose(1, 2, 0, 3)
    send = jnp.concatenate([q, kv], axis=1).reshape(F, 1, C, 5, 4, HALF * NOPE)
    send = jnp.broadcast_to(send, (F, ZH, C, 5, 4, HALF * NOPE)).reshape(F * ZH * C, 5, 4, -1)
    part = lax.all_to_all(send, ("zl", "y", "zh", "c"), split_axis=0, concat_axis=0, tiled=True)
    part = part.reshape(F, ZH * C, 5, 4, HALF * NOPE)
    part_q = part[:, :, :3].reshape(F, Q_BLOCK, HALF * NOPE)
    part_kv = part[:, :, 3:].transpose(0, 2, 1, 3, 4).reshape(F, 2 * L_BLOCK, HALF * NOPE)
    message = jnp.concatenate([part_q, part_kv], axis=1)

    own = [message] + [None] * 3
    for d in (2, 1, 3):
        own[d] = over(message, d, 0, 0)
    o_x = jnp.stack([o_x[d] for d in range(X)])
    half = lambda z: lax.dynamic_slice_in_dim(o_x, z * (2 * D_PART), 2 * D_PART, 2)
    o_own = half(zh)
    o_other = over(half(1 - zh), 0, 1, 0)
    o_parts = [o_own, o_other, over(o_own, 0, 0, 1), over(o_other, 0, 0, 1)]
    other = [over(m, 0, 0, 1) for m in own]

    scalars = lambda base: jnp.stack([x, zh, c, base]).astype(jnp.int32)
    first = absorb(scalars(HALF * c), own, o_parts)
    q_absorbed, d_out = absorb(scalars(HALF * (1 - c)), other, o_parts, first)
    return q_absorbed, d_out.transpose(0, 2, 1)


def solution(mesh):
    fine = Mesh(mesh.devices.reshape(ZL, Y, X, ZH, C), ("zl", "y", "x", "zh", "c"))
    rows = P(("zl", "y", "x", "zh", "c"), None)
    return jax.shard_map(
        on_device,
        mesh=fine,
        in_specs=(rows, rows, rows),
        out_specs=(P(("zl", "y"), None, None), P(("zl", "y"), None, BULK)),
        check_vma=False,
    )
```

```python
import functools

import jax
import jax.numpy as jnp
from jax import lax
from jax.experimental import pallas as pl
from jax.experimental.pallas import tpu as pltpu
from jax.sharding import Mesh, PartitionSpec as P

QL = 1536
KVL = 512
NOPE = 128
VD = 128
X, ZH, ZL, Y, C = 4, 2, 2, 4, 2
BULK = ("x", "zh", "c")
OWNERS = ("zl", "y", "zh", "c")
F = ZL * Y
HEADS = 8
HALF = 4
WIDE = HALF * NOPE
Q_ROWS, KV_ROWS = 12, 4
Q_BLOCK = ZH * C * Q_ROWS
Q_ALL = F * Q_BLOCK
L_BLOCK = ZH * C * KV_ROWS
SPLIT = (Q_ALL + 2 * F * L_BLOCK) // 2
D_PART = 448
bf16 = jnp.bfloat16
PACK_MIB = 56
VMEM = pl.BlockSpec(memory_space=pltpu.VMEM)
ANY = pl.BlockSpec(memory_space=pl.ANY)


def shifts(dx, dz, dc):
    at = lambda x, z, c: (x * ZH + z) * C + c
    return [
        (at(x, z, c), at((x + dx) % X, (z + dz) % ZH, (c + dc) % C))
        for x in range(X)
        for z in range(ZH)
        for c in range(C)
    ]


COST = pl.CostEstimate(flops=1024, bytes_accessed=1024, transcendentals=0)


def limit(mib):
    return pltpu.CompilerParams(vmem_limit_bytes=mib * 2**20)


def pack_kernel(q_hbm, kv_hbm, o_hbm, out_ref, *refs):
    o_refs, (q_ref, kv_ref, sems) = refs[:X], refs[X:]
    kv_copy = pltpu.make_async_copy(kv_hbm, kv_ref, sems.at[0])
    q_copy = pltpu.make_async_copy(q_hbm, q_ref, sems.at[1])
    kv_copy.start()
    q_copy.start()
    copies = []
    o_cols = o_hbm.shape[1] // X
    for d in range(X):
        at = pl.multiple_of(lax.rem(lax.axis_index("x") + d, X) * o_cols, 128)
        copies.append(
            pltpu.make_async_copy(o_hbm.at[:, pl.ds(at, o_cols)], o_refs[d], sems.at[2 + d])
        )
        copies[d].start()
    kv_copy.wait()
    for n in range(F * C):
        for z in range(ZH):
            at = (n // C * ZH + z) * C + n % C
            out_ref[at, Q_ROWS:, :WIDE] = kv_ref[:, n * 1024 : n * 1024 + WIDE]
            for j in range(4):
                lane = n * 1024 + WIDE + j * 128
                out_ref[at, j * 4 : (j + 1) * 4, WIDE:] = kv_ref[:, lane : lane + 128]
    q_copy.wait()
    for n in range(F * C):
        for z in range(ZH):
            at = (n // C * ZH + z) * C + n % C
            out_ref[at, :Q_ROWS, :WIDE] = q_ref[:, n * WIDE : (n + 1) * WIDE]
    for copy in copies:
        copy.wait()


def pack(q, kv, o):
    o_cols = o.shape[1] // X
    out = pl.pallas_call(
        pack_kernel,
        in_specs=[ANY] * 3,
        out_specs=[VMEM] * (X + 1),
        out_shape=[jax.ShapeDtypeStruct((F * ZH * C, 16, 640), bf16)]
        + [jax.ShapeDtypeStruct((o.shape[0], o_cols), bf16)] * X,
        scratch_shapes=[
            pltpu.VMEM(q.shape, bf16),
            pltpu.VMEM(kv.shape, bf16),
            pltpu.SemaphoreType.DMA((2 + X,)),
        ],
        compiler_params=limit(PACK_MIB),
        cost_estimate=COST,
    )(q, kv, o)
    return out[0], out[1:]


def unpack_kernel(packed_ref, left_ref, right_ref, first, second):
    half_q, half_l = F // 2 * Q_BLOCK, F // 2 * L_BLOCK

    def put(at, block):
        cut = max(0, min(block.shape[0], SPLIT - at))
        if cut:
            first[at : at + cut, : block.shape[1]] = block[:cut]
        if cut < block.shape[0]:
            second[at + cut - SPLIT : at + block.shape[0] - SPLIT] = block[cut:]

    for g in range(2):
        packed = packed_ref[g * 256 : (g + 1) * 256]
        left = jnp.dot(left_ref[...], packed[:, :WIDE], preferred_element_type=jnp.float32)
        right = jnp.dot(right_ref[...], packed[:, WIDE:], preferred_element_type=jnp.float32)
        left, right = left.astype(bf16), right.astype(bf16)
        put(g * half_q, left[:half_q])
        put(Q_ALL + g * half_l, left[half_q:])
        at = Q_ALL + g * half_l + F * L_BLOCK
        lanes = [right[j * half_l : (j + 1) * half_l] for j in range(4)]
        put(at, jnp.concatenate(lanes, axis=1))


def unpack(packed):
    row, column = jnp.arange(256), jnp.arange(256)[None, :]
    of_q = row // Q_ROWS * 16 + row % Q_ROWS
    r = row % 64
    of_kv = r // KV_ROWS * 16 + r % KV_ROWS
    left = jnp.where(row < 192, of_q, of_kv + Q_ROWS)
    right = of_kv + row // 64 * 4
    select = lambda source: (source[:, None] == column).astype(bf16)
    return pl.pallas_call(
        unpack_kernel,
        out_shape=[jax.ShapeDtypeStruct((SPLIT, WIDE), bf16)] * 2,
        compiler_params=limit(8),
        cost_estimate=COST,
    )(packed, select(left), select(right))


def sort_kernel(*refs):
    parts, out, kv = refs[: 2 * X], refs[2 * X], refs[2 * X + 1]
    for d in range(X):
        first, second = parts[2 * d], parts[2 * d + 1]
        xs = lax.rem(lax.axis_index("x") - d + X, X)
        for f in range(F):
            at = pl.multiple_of(f * (X * L_BLOCK) + xs * L_BLOCK, L_BLOCK)
            for h in range(2):
                source = Q_ALL + (h * F + f) * L_BLOCK - SPLIT
                rows = second[source : source + L_BLOCK]
                kv[pl.ds(at, L_BLOCK), h * WIDE : (h + 1) * WIDE] = rows
        at = 2 * KVL + d * Q_ALL
        out[at : at + SPLIT] = first[...]
        out[at + SPLIT : at + Q_ALL] = second[: Q_ALL - SPLIT]
    for k in range(HALF):
        out[k * NOPE : (k + 1) * NOPE] = kv[:, k * 256 : k * 256 + NOPE].T
        out[KVL : 2 * KVL, k * VD : (k + 1) * VD] = kv[:, k * 256 + NOPE : (k + 1) * 256]


def sort_rows(parts):
    return pl.pallas_call(
        sort_kernel,
        in_specs=[VMEM] * (2 * X),
        out_specs=VMEM,
        out_shape=jax.ShapeDtypeStruct((2 * KVL + X * Q_ALL, WIDE), bf16),
        scratch_shapes=[pltpu.VMEM((KVL, 1024), bf16)],
        compiler_params=limit(12),
        cost_estimate=COST,
    )(*parts)


def sender(sems):
    copies = []

    def send(source, target):
        copy = pltpu.make_async_copy(source, target, sems.at[len(copies)])
        copy.start()
        copies.append(copy)

    return copies, send


def query_blocks(x, half, rows_ref, q_out, blocks, send):
    for d in range(X):
        xs = lax.rem(x - d + X, X)
        first = 2 * KVL + d * Q_ALL
        for k in range(HALF):
            lanes = slice(k * NOPE, (k + 1) * NOPE)
            block = jnp.dot(
                rows_ref[first : first + Q_ALL, lanes],
                rows_ref[lanes],
                preferred_element_type=jnp.float32,
            )
            at = d * HALF + k
            blocks[at] = block.astype(bf16).reshape(F, Q_BLOCK, KVL)
            send(blocks.at[at], q_out.at[half * HALF + k, :, xs])


def absorb_kernel(mine, *refs):
    rows_ref, own_refs, other_refs = refs[0], refs[1:3], refs[3:5]
    q_out, d_out, blocks, heads, wide, sems = refs[-6:]
    x, zh, c = (lax.axis_index(a) for a in BULK)
    half = c if mine else 1 - c
    copies, send = sender(sems)
    query_blocks(x, half, rows_ref, q_out, blocks, send)
    lanes = pl.ds(pl.multiple_of(c * 384, 128), 512)
    own_at = pl.ds(pl.multiple_of(c * 64, 64), 64)
    other_at = pl.ds(pl.multiple_of((1 - c) * 64, 64), 64)
    part = pl.ds(pl.multiple_of(c * 64, 64), D_PART)
    for k in range(HALF):
        d = lax.rem(x - (2 * half + k // 2) + X, X)
        for z in range(ZH):

            @pl.when(lax.rem(zh + k, ZH) == z)
            def _():
                heads[k, own_at, :] = own_refs[z][d, :, lanes]
                heads[k, other_at, :] = other_refs[z][d, :, lanes]

    for k in range(HALF):
        value = rows_ref[KVL : 2 * KVL, k * VD : (k + 1) * VD]
        wide[k] = lax.dot_general(
            heads[k], value, (((0,), (1,)), ((), ())), preferred_element_type=jnp.float32
        ).astype(bf16)
        send(wide.at[k, part], d_out.at[half * HALF + k])
    for copy in copies:
        copy.wait()


def absorb(mine, rows, o_own, o_other, earlier=()):
    return pl.pallas_call(
        functools.partial(absorb_kernel, mine),
        in_specs=[VMEM] * 5 + [ANY] * len(earlier),
        out_specs=[ANY, ANY],
        scratch_shapes=[
            pltpu.VMEM((X * HALF, F, Q_BLOCK, KVL), bf16),
            pltpu.VMEM((HALF, VD, 512), bf16),
            pltpu.VMEM((HALF, 512, KVL), bf16),
            pltpu.SemaphoreType.DMA((X * HALF + HALF,)),
        ],
        out_shape=[
            jax.ShapeDtypeStruct((HEADS, F, X, Q_BLOCK, KVL), bf16),
            jax.ShapeDtypeStruct((HEADS, D_PART, KVL), bf16),
        ],
        input_output_aliases={5: 0, 6: 1} if earlier else {},
        compiler_params=limit(20),
        cost_estimate=COST,
    )(rows, *o_own, *o_other, *earlier)


def on_device(q_nope, kv_up, o_proj):
    zh = lax.axis_index("zh")
    over = lambda a, *d: lax.ppermute(a, BULK, shifts(*d))
    core = (0, 0, 1)

    packed, o_send = pack(q_nope, kv_up, o_proj)
    packed = lax.all_to_all(packed, OWNERS, split_axis=0, concat_axis=0, tiled=True)
    o_x = [o_send[0]] + [over(o_send[d], d, 0, 0) for d in (1, 2, 3)]
    packed, o_x = lax.optimization_barrier((packed, o_x))

    right, left = (1, 0, 0), (3, 0, 0)
    own = unpack(packed.reshape(F * ZH * C * 16, 640))
    from_left, from_right = [over(own[0], *right)], [over(own[1], *left)]
    from_left.append(over(own[1], *right))
    from_right.insert(0, over(own[0], *left))
    far = [over(from_left[0], *right), over(from_right[1], *left)]
    o_x = jnp.stack(o_x)
    half = lambda z: lax.dynamic_slice_in_dim(o_x, z * (2 * D_PART), 2 * D_PART, 2)
    o_own = [half(zh), over(half(1 - zh), 0, 1, 0)]
    o_other = [over(o, *core) for o in o_own]
    arrived = [*from_left, *far, *from_right]
    arrived, o_own, o_other = lax.optimization_barrier((arrived, o_own, o_other))

    rows = sort_rows([*own, *arrived])
    rows_other = over(rows, *core)
    outs = absorb(True, rows, o_own, o_other)
    q_out, d_out = absorb(False, rows_other, o_own, o_other, outs)
    return q_out.reshape(HEADS, QL, KVL), d_out.transpose(0, 2, 1)


def solution(mesh):
    fine = Mesh(mesh.devices.reshape(ZL, Y, X, ZH, C), ("zl", "y", "x", "zh", "c"))
    rows = P(("zl", "y", "x", "zh", "c"), None)
    return jax.shard_map(
        on_device,
        mesh=fine,
        in_specs=(rows, rows, rows),
        out_specs=(P(("zl", "y"), None, None), P(("zl", "y"), None, BULK)),
        check_vma=False,
    )
```

```python
import jax
import jax.numpy as jnp
from jax import lax
from jax.experimental import pallas as pl
from jax.experimental.pallas import tpu as pltpu
from jax.sharding import Mesh, PartitionSpec as P

QL = 1536
KVL = 512
NOPE = 128
VD = 128
X, ZH, ZL, Y, C = 4, 2, 2, 4, 2
BULK = ("x", "zh", "c")
OWNERS = ("zl", "y", "zh", "c")
F = ZL * Y
HEADS = 8
HALF = 4
WIDE = HALF * NOPE
Q_ROWS, KV_ROWS = 12, 4
Q_BLOCK = ZH * C * Q_ROWS
Q_ALL = F * Q_BLOCK
L_BLOCK = ZH * C * KV_ROWS
ROWS = Q_ALL + 2 * F * L_BLOCK
D_PART = 448
bf16 = jnp.bfloat16
PACK_MIB = 56
EXTRA = 48
VMEM = pl.BlockSpec(memory_space=pltpu.VMEM)
ANY = pl.BlockSpec(memory_space=pl.ANY)


def shifts(dx, dz, dc):
    at = lambda x, z, c: (x * ZH + z) * C + c
    return [
        (at(x, z, c), at((x + dx) % X, (z + dz) % ZH, (c + dc) % C))
        for x in range(X)
        for z in range(ZH)
        for c in range(C)
    ]


COST = pl.CostEstimate(flops=1024, bytes_accessed=1024, transcendentals=0)


def limit(mib):
    return pltpu.CompilerParams(vmem_limit_bytes=mib * 2**20)


def pack_kernel(q_hbm, kv_hbm, o_hbm, out_ref, *refs):
    o_refs, (q_ref, kv_ref, sems) = refs[:X], refs[X:]
    kv_copy = pltpu.make_async_copy(kv_hbm, kv_ref, sems.at[0])
    q_copy = pltpu.make_async_copy(q_hbm, q_ref, sems.at[1])
    kv_copy.start()
    q_copy.start()
    copies = []
    o_cols = o_hbm.shape[1] // X
    for d in range(X):
        at = pl.multiple_of(lax.rem(lax.axis_index("x") + d, X) * o_cols, 128)
        copies.append(
            pltpu.make_async_copy(o_hbm.at[:, pl.ds(at, o_cols)], o_refs[d], sems.at[2 + d])
        )
        copies[d].start()
    kv_copy.wait()
    for n in range(F * C):
        for z in range(ZH):
            at = (n // C * ZH + z) * C + n % C
            out_ref[at, Q_ROWS:, :WIDE] = kv_ref[:, n * 1024 : n * 1024 + WIDE]
            for j in range(4):
                lane = n * 1024 + WIDE + j * 128
                out_ref[at, j * 4 : (j + 1) * 4, WIDE:] = kv_ref[:, lane : lane + 128]
    q_copy.wait()
    for n in range(F * C):
        for z in range(ZH):
            at = (n // C * ZH + z) * C + n % C
            out_ref[at, :Q_ROWS, :WIDE] = q_ref[:, n * WIDE : (n + 1) * WIDE]
    for copy in copies:
        copy.wait()


def pack(q, kv, o):
    o_cols = o.shape[1] // X
    out = pl.pallas_call(
        pack_kernel,
        in_specs=[ANY] * 3,
        out_specs=[VMEM] * (X + 1),
        out_shape=[jax.ShapeDtypeStruct((F * ZH * C, 16, 640), bf16)]
        + [jax.ShapeDtypeStruct((o.shape[0], o_cols), bf16)] * X,
        scratch_shapes=[
            pltpu.VMEM(q.shape, bf16),
            pltpu.VMEM(kv.shape, bf16),
            pltpu.SemaphoreType.DMA((2 + X,)),
        ],
        compiler_params=limit(PACK_MIB),
        cost_estimate=COST,
    )(q, kv, o)
    return out[0], out[1:]


def unpack_kernel(packed_ref, left_ref, right_ref, half_left_ref, half_right_ref, out, half_out):
    half_out[ROWS // 2 :] = jnp.zeros((EXTRA, WIDE), bf16)
    for g in range(2):
        packed = packed_ref[g * 256 : (g + 1) * 256]
        for left_by, right_by, ref in (
            (left_ref, right_ref, out),
            (half_left_ref, half_right_ref, half_out),
        ):
            left = jnp.dot(left_by[...], packed[:, :WIDE], preferred_element_type=jnp.float32)
            right = jnp.dot(right_by[...], packed[:, WIDE:], preferred_element_type=jnp.float32)
            left, right = left.astype(bf16), right.astype(bf16)
            rows_l = left_by.shape[0] // 4
            rows_q = 3 * rows_l
            ref[g * rows_q : (g + 1) * rows_q] = left[:rows_q]
            at = (2 * 3 + g) * rows_l
            ref[at : at + rows_l] = left[rows_q:]
            at += 2 * rows_l
            for j in range(4):
                lanes = slice(j * 128, (j + 1) * 128)
                ref[at : at + rows_l, lanes] = right[j * rows_l : (j + 1) * rows_l]


def unpack(packed, zh):
    column = jnp.arange(256)[None, :]

    def select(sources, first):
        size = sources * 16
        row = jnp.arange(4 * size)
        block = lambda n: n // sources * 4 + n % sources + first
        of_q = block(row // Q_ROWS) * 16 + row % Q_ROWS
        r = row % size
        of_kv = block(r // KV_ROWS) * 16 + r % KV_ROWS
        left = jnp.where(row < 3 * size, of_q, of_kv + Q_ROWS)
        right = of_kv + row // size * 4
        return [(source[:, None] == column).astype(bf16) for source in (left, right)]

    return pl.pallas_call(
        unpack_kernel,
        out_shape=[
            jax.ShapeDtypeStruct((ROWS, WIDE), bf16),
            jax.ShapeDtypeStruct((ROWS // 2 + EXTRA, WIDE), bf16),
        ],
        compiler_params=limit(8),
        cost_estimate=COST,
    )(packed, *select(4, 0), *select(2, zh * 2))


def sort_kernel(own, right, left, same_ref, cross_ref, by_q_ref, by_l_ref, out, far, kv):
    half_q, half_l = Q_ALL // 4, F * L_BLOCK // 2
    for g in range(2):
        at = slice(g * half_q, (g + 1) * half_q)
        block = jnp.concatenate([same_ref[at], cross_ref[at]], axis=0)
        block = jnp.dot(by_q_ref[...], block, preferred_element_type=jnp.float32)
        far[2 * g * half_q : 2 * (g + 1) * half_q] = block.astype(bf16)
    for h in range(2):
        at = slice(Q_ALL // 2 + h * half_l, Q_ALL // 2 + (h + 1) * half_l)
        block = jnp.concatenate([same_ref[at], cross_ref[at]], axis=0)
        block = jnp.dot(by_l_ref[...], block, preferred_element_type=jnp.float32)
        at = Q_ALL + 2 * h * half_l
        far[at : at + 2 * half_l] = block.astype(bf16)
    for d, ref in enumerate((own, right, far, left)):
        xs = lax.rem(lax.axis_index("x") - d + X, X)
        for f in range(F):
            at = pl.multiple_of(f * (X * L_BLOCK) + xs * L_BLOCK, L_BLOCK)
            for h in range(2):
                source = Q_ALL + (h * F + f) * L_BLOCK
                rows = ref[source : source + L_BLOCK]
                kv[pl.ds(at, L_BLOCK), h * WIDE : (h + 1) * WIDE] = rows
        out[2 * KVL + d * Q_ALL : 2 * KVL + (d + 1) * Q_ALL] = ref[:Q_ALL]
    for k in range(HALF):
        out[k * NOPE : (k + 1) * NOPE] = kv[:, k * 256 : k * 256 + NOPE].T
        out[KVL : 2 * KVL, k * VD : (k + 1) * VD] = kv[:, k * 256 + NOPE : (k + 1) * 256]


def interleave(blocks, size, zh):
    row = jnp.arange(2 * blocks * size)
    z = row // size % ZH
    source = jnp.where(z == zh, 0, blocks * size) + row // (ZH * size) * size + row % size
    return (source[:, None] == row[None, :]).astype(bf16)


def sort_rows(zh, own, right, left, same, cross):
    return pl.pallas_call(
        sort_kernel,
        out_shape=jax.ShapeDtypeStruct((2 * KVL + X * Q_ALL, WIDE), bf16),
        scratch_shapes=[pltpu.VMEM((ROWS, WIDE), bf16), pltpu.VMEM((KVL, 1024), bf16)],
        compiler_params=limit(12),
        cost_estimate=COST,
    )(own, right, left, same, cross, interleave(F // 2, 24, zh), interleave(F, 8, zh))


def sender(sems):
    copies = []

    def send(source, target):
        copy = pltpu.make_async_copy(source, target, sems.at[len(copies)])
        copy.start()
        copies.append(copy)

    return copies, send


def query_blocks(x, half, rows_ref, q_out, blocks, send):
    for d in range(X):
        xs = lax.rem(x - d + X, X)
        first = 2 * KVL + d * Q_ALL
        for k in range(HALF):
            lanes = slice(k * NOPE, (k + 1) * NOPE)
            block = jnp.dot(
                rows_ref[first : first + Q_ALL, lanes],
                rows_ref[lanes],
                preferred_element_type=jnp.float32,
            )
            at = d * HALF + k
            blocks[at] = block.astype(bf16).reshape(F, Q_BLOCK, KVL)
            send(blocks.at[at], q_out.at[half * HALF + k, :, xs])


def query_kernel(rows_ref, q_out, blocks, sems):
    copies, send = sender(sems)
    query_blocks(lax.axis_index("x"), lax.axis_index("c"), rows_ref, q_out, blocks, send)
    for copy in copies:
        copy.wait()


def query(rows):
    return pl.pallas_call(
        query_kernel,
        in_specs=[VMEM],
        out_specs=ANY,
        scratch_shapes=[
            pltpu.VMEM((X * HALF, F, Q_BLOCK, KVL), bf16),
            pltpu.SemaphoreType.DMA((X * HALF,)),
        ],
        out_shape=jax.ShapeDtypeStruct((HEADS, F, X, Q_BLOCK, KVL), bf16),
        compiler_params=limit(16),
        cost_estimate=COST,
    )(rows)


def rest_kernel(own_ref, other_ref, o_own_ref, o_other_ref, _, q_out, d_out, *scratch):
    blocks, heads, wide, sems = scratch
    x, zh, c = (lax.axis_index(a) for a in BULK)
    copies, send = sender(sems)
    lanes = pl.ds(pl.multiple_of(c * 384, 128), 512)
    own_at = pl.ds(pl.multiple_of(c * 64, 64), 64)
    other_at = pl.ds(pl.multiple_of((1 - c) * 64, 64), 64)
    part = pl.ds(pl.multiple_of(c * 64, 64), D_PART)
    query_blocks(x, 1 - c, other_ref, q_out, blocks, send)
    for n, (rows_ref, half) in enumerate(((own_ref, c), (other_ref, 1 - c))):
        for k in range(HALF):
            d = lax.rem(x - (2 * half + k // 2) + X, X)
            z = lax.rem(zh + k, 2)
            at = n * HALF + k
            heads[at, own_at, :] = o_own_ref[z, d, :, lanes]
            heads[at, other_at, :] = o_other_ref[z, d, :, lanes]
        for k in range(HALF):
            at = n * HALF + k
            value = rows_ref[KVL : 2 * KVL, k * VD : (k + 1) * VD]
            wide[at] = lax.dot_general(
                heads[at], value, (((0,), (1,)), ((), ())), preferred_element_type=jnp.float32
            ).astype(bf16)
            send(wide.at[at, part], d_out.at[half * HALF + k])
    for copy in copies:
        copy.wait()


def rest(rows, rows_other, o_own, o_other, q_out):
    return pl.pallas_call(
        rest_kernel,
        in_specs=[VMEM] * 4 + [ANY],
        out_specs=[ANY, ANY],
        scratch_shapes=[
            pltpu.VMEM((X * HALF, F, Q_BLOCK, KVL), bf16),
            pltpu.VMEM((HEADS, VD, 512), bf16),
            pltpu.VMEM((HEADS, 512, KVL), bf16),
            pltpu.SemaphoreType.DMA((X * HALF + HEADS,)),
        ],
        out_shape=[
            jax.ShapeDtypeStruct((HEADS, F, X, Q_BLOCK, KVL), bf16),
            jax.ShapeDtypeStruct((HEADS, D_PART, KVL), bf16),
        ],
        input_output_aliases={4: 0},
        compiler_params=limit(20),
        cost_estimate=COST,
    )(rows, rows_other, o_own, o_other, q_out)


def on_device(q_nope, kv_up, o_proj):
    zh = lax.axis_index("zh")
    over = lambda a, *d: lax.ppermute(a, BULK, shifts(*d))
    core = (0, 0, 1)

    packed, o_send = pack(q_nope, kv_up, o_proj)
    packed = lax.all_to_all(packed, OWNERS, split_axis=0, concat_axis=0, tiled=True)
    o_x = [o_send[0]] + [over(o_send[d], d, 0, 0) for d in (1, 2, 3)]
    packed, o_x = lax.optimization_barrier((packed, o_x))

    own, part = unpack(packed.reshape(F * ZH * C * 16, 640), zh)
    same = over(part, 2, 0, 0)
    near = [over(own, 1, 0, 0), over(own, 3, 0, 0)]
    cross = over(same, 0, 1, 0)
    half = lambda z: jnp.stack(
        [lax.dynamic_slice_in_dim(o, z * (2 * D_PART), 2 * D_PART, 1) for o in o_x]
    )
    o_z = over(half(1 - zh), 0, 1, 0)
    near, same, cross, o_z = lax.optimization_barrier((near, same, cross, o_z))

    o_own = jnp.stack([half(zh), o_z])
    o_other = over(o_own, *core)
    rows = sort_rows(zh, own, *near, same, cross)
    rows_other = over(rows, *core)
    q_out = query(rows)
    q_out, d_out = rest(rows, rows_other, o_own, o_other, q_out)
    return q_out.reshape(HEADS, QL, KVL), d_out.transpose(0, 2, 1)


def solution(mesh):
    fine = Mesh(mesh.devices.reshape(ZL, Y, X, ZH, C), ("zl", "y", "x", "zh", "c"))
    rows = P(("zl", "y", "x", "zh", "c"), None)
    return jax.shard_map(
        on_device,
        mesh=fine,
        in_specs=(rows, rows, rows),
        out_specs=(P(("zl", "y"), None, None), P(("zl", "y"), None, BULK)),
        check_vma=False,
    )
```

```python
import jax
import jax.numpy as jnp
from jax import lax
from jax.experimental import pallas as pl
from jax.experimental.pallas import tpu as pltpu
from jax.sharding import Mesh, PartitionSpec as P

QL = 1536
KVL = 512
NOPE = 128
VD = 128
X, ZH, ZL, Y, C = 4, 2, 2, 4, 2
BULK = ("x", "zh", "c")
OWNERS = ("zl", "y", "zh", "c")
F = ZL * Y
HEADS = 8
HALF = 4
WIDE = HALF * NOPE
Q_ROWS, KV_ROWS = 12, 4
Q_BLOCK = ZH * C * Q_ROWS
Q_ALL = F * Q_BLOCK
L_BLOCK = ZH * C * KV_ROWS
ROWS = Q_ALL + 2 * F * L_BLOCK
D_PART = 448
bf16 = jnp.bfloat16
PACK_MIB = 24
EXTRA = 48
VMEM = pl.BlockSpec(memory_space=pltpu.VMEM)
ANY = pl.BlockSpec(memory_space=pl.ANY)


def shifts(dx, dz, dc):
    at = lambda x, z, c: (x * ZH + z) * C + c
    return [
        (at(x, z, c), at((x + dx) % X, (z + dz) % ZH, (c + dc) % C))
        for x in range(X)
        for z in range(ZH)
        for c in range(C)
    ]


COST = pl.CostEstimate(flops=1024, bytes_accessed=1024, transcendentals=0)


def limit(mib):
    return pltpu.CompilerParams(vmem_limit_bytes=mib * 2**20)


def pack_kernel(q_ref, kv_ref, o_hbm, out_ref, *refs):
    o_refs, sems = refs[:X], refs[X]
    copies = []
    o_cols = o_hbm.shape[1] // X
    for d in range(X):
        at = pl.multiple_of(lax.rem(lax.axis_index("x") + d, X) * o_cols, 128)
        copies.append(
            pltpu.make_async_copy(o_hbm.at[:, pl.ds(at, o_cols)], o_refs[d], sems.at[d])
        )
        copies[d].start()
    for n in range(F * C):
        first = n // C * (ZH * C) + n % C
        q_lanes = slice(n * WIDE, (n + 1) * WIDE)
        for at in (first, first + C):
            out_ref[at, :Q_ROWS, :WIDE] = q_ref[:, q_lanes]
            out_ref[at, Q_ROWS:, :WIDE] = kv_ref[:, n * 1024 : n * 1024 + WIDE]
            for j in range(4):
                lane = n * 1024 + WIDE + j * 128
                out_ref[at, j * 4 : (j + 1) * 4, WIDE:] = kv_ref[:, lane : lane + 128]
    for copy in copies:
        copy.wait()


def pack(q, kv, o):
    o_cols = o.shape[1] // X
    out = pl.pallas_call(
        pack_kernel,
        in_specs=[VMEM, VMEM, ANY],
        out_specs=[VMEM] * (X + 1),
        out_shape=[jax.ShapeDtypeStruct((F * ZH * C, 16, 640), bf16)]
        + [jax.ShapeDtypeStruct((o.shape[0], o_cols), bf16)] * X,
        scratch_shapes=[pltpu.SemaphoreType.DMA((X,))],
        compiler_params=limit(PACK_MIB),
        cost_estimate=COST,
    )(q, kv, o)
    return out[0], out[1:]


def unpack_kernel(packed_ref, left_ref, right_ref, half_left_ref, half_right_ref, out, half_out):
    half_out[ROWS // 2 :] = jnp.zeros((EXTRA, WIDE), bf16)
    for g in range(2):
        packed = packed_ref[g * 256 : (g + 1) * 256]
        for left_by, right_by, ref in (
            (left_ref, right_ref, out),
            (half_left_ref, half_right_ref, half_out),
        ):
            left = jnp.dot(left_by[...], packed[:, :WIDE], preferred_element_type=jnp.float32)
            right = jnp.dot(right_by[...], packed[:, WIDE:], preferred_element_type=jnp.float32)
            left, right = left.astype(bf16), right.astype(bf16)
            rows_l = left_by.shape[0] // 4
            rows_q = 3 * rows_l
            ref[g * rows_q : (g + 1) * rows_q] = left[:rows_q]
            at = (2 * 3 + g) * rows_l
            ref[at : at + rows_l] = left[rows_q:]
            at += 2 * rows_l
            for j in range(4):
                lanes = slice(j * 128, (j + 1) * 128)
                ref[at : at + rows_l, lanes] = right[j * rows_l : (j + 1) * rows_l]


def unpack(packed, zh):
    column = jnp.arange(256)[None, :]

    def select(sources, first):
        size = sources * 16
        row = jnp.arange(4 * size)
        block = lambda n: n // sources * 4 + n % sources + first
        of_q = block(row // Q_ROWS) * 16 + row % Q_ROWS
        r = row % size
        of_kv = block(r // KV_ROWS) * 16 + r % KV_ROWS
        left = jnp.where(row < 3 * size, of_q, of_kv + Q_ROWS)
        right = of_kv + row // size * 4
        return [(source[:, None] == column).astype(bf16) for source in (left, right)]

    return pl.pallas_call(
        unpack_kernel,
        out_shape=[
            jax.ShapeDtypeStruct((ROWS, WIDE), bf16),
            jax.ShapeDtypeStruct((ROWS // 2 + EXTRA, WIDE), bf16),
        ],
        compiler_params=limit(8),
        cost_estimate=COST,
    )(packed, *select(4, 0), *select(2, zh * 2))


def sort_kernel(own, right, left, same_ref, cross_ref, by_q_ref, by_l_ref, out, far, kv):
    half_q, half_l = Q_ALL // 4, F * L_BLOCK // 2
    for g in range(2):
        at = slice(g * half_q, (g + 1) * half_q)
        block = jnp.concatenate([same_ref[at], cross_ref[at]], axis=0)
        block = jnp.dot(by_q_ref[...], block, preferred_element_type=jnp.float32)
        far[2 * g * half_q : 2 * (g + 1) * half_q] = block.astype(bf16)
    for h in range(2):
        at = slice(Q_ALL // 2 + h * half_l, Q_ALL // 2 + (h + 1) * half_l)
        block = jnp.concatenate([same_ref[at], cross_ref[at]], axis=0)
        block = jnp.dot(by_l_ref[...], block, preferred_element_type=jnp.float32)
        at = Q_ALL + 2 * h * half_l
        far[at : at + 2 * half_l] = block.astype(bf16)
    for d, ref in enumerate((own, right, far, left)):
        xs = lax.rem(lax.axis_index("x") - d + X, X)
        for f in range(F):
            at = pl.multiple_of(f * (X * L_BLOCK) + xs * L_BLOCK, L_BLOCK)
            for h in range(2):
                source = Q_ALL + (h * F + f) * L_BLOCK
                rows = ref[source : source + L_BLOCK]
                kv[pl.ds(at, L_BLOCK), h * WIDE : (h + 1) * WIDE] = rows
        out[2 * KVL + d * Q_ALL : 2 * KVL + (d + 1) * Q_ALL] = ref[:Q_ALL]
    for k in range(HALF):
        out[k * NOPE : (k + 1) * NOPE] = kv[:, k * 256 : k * 256 + NOPE].T
        out[KVL : 2 * KVL, k * VD : (k + 1) * VD] = kv[:, k * 256 + NOPE : (k + 1) * 256]


def interleave(blocks, size, zh):
    row = jnp.arange(2 * blocks * size)
    z = row // size % ZH
    source = jnp.where(z == zh, 0, blocks * size) + row // (ZH * size) * size + row % size
    return (source[:, None] == row[None, :]).astype(bf16)


def sort_rows(zh, own, right, left, same, cross):
    return pl.pallas_call(
        sort_kernel,
        out_shape=jax.ShapeDtypeStruct((2 * KVL + X * Q_ALL, WIDE), bf16),
        scratch_shapes=[pltpu.VMEM((ROWS, WIDE), bf16), pltpu.VMEM((KVL, 1024), bf16)],
        compiler_params=limit(12),
        cost_estimate=COST,
    )(own, right, left, same, cross, interleave(F // 2, 24, zh), interleave(F, 8, zh))


def sender(sems):
    copies = []

    def send(source, target):
        copy = pltpu.make_async_copy(source, target, sems.at[len(copies)])
        copy.start()
        copies.append(copy)

    return copies, send


def query_blocks(x, half, rows_ref, q_out, blocks, send):
    for d in range(X):
        xs = lax.rem(x - d + X, X)
        first = 2 * KVL + d * Q_ALL
        for k in range(HALF):
            lanes = slice(k * NOPE, (k + 1) * NOPE)
            block = jnp.dot(
                rows_ref[first : first + Q_ALL, lanes],
                rows_ref[lanes],
                preferred_element_type=jnp.float32,
            )
            at = d * HALF + k
            blocks[at] = block.astype(bf16).reshape(F, Q_BLOCK, KVL)
            send(blocks.at[at], q_out.at[half * HALF + k, :, xs])


def query_kernel(rows_ref, q_out, blocks, sems):
    copies, send = sender(sems)
    query_blocks(lax.axis_index("x"), lax.axis_index("c"), rows_ref, q_out, blocks, send)
    for copy in copies:
        copy.wait()


def query(rows):
    return pl.pallas_call(
        query_kernel,
        in_specs=[VMEM],
        out_specs=ANY,
        scratch_shapes=[
            pltpu.VMEM((X * HALF, F, Q_BLOCK, KVL), bf16),
            pltpu.SemaphoreType.DMA((X * HALF,)),
        ],
        out_shape=jax.ShapeDtypeStruct((HEADS, F, X, Q_BLOCK, KVL), bf16),
        compiler_params=limit(16),
        cost_estimate=COST,
    )(rows)


def rest_kernel(own_ref, other_ref, o_own_ref, o_other_ref, _, q_out, d_out, *scratch):
    blocks, heads, wide, sems = scratch
    x, zh, c = (lax.axis_index(a) for a in BULK)
    copies, send = sender(sems)
    lanes = pl.ds(pl.multiple_of(c * 384, 128), 512)
    own_at = pl.ds(pl.multiple_of(c * 64, 64), 64)
    other_at = pl.ds(pl.multiple_of((1 - c) * 64, 64), 64)
    part = pl.ds(pl.multiple_of(c * 64, 64), D_PART)
    query_blocks(x, 1 - c, other_ref, q_out, blocks, send)
    for n, (rows_ref, half) in enumerate(((own_ref, c), (other_ref, 1 - c))):
        for k in range(HALF):
            d = lax.rem(x - (2 * half + k // 2) + X, X)
            z = lax.rem(zh + k, 2)
            at = n * HALF + k
            heads[at, own_at, :] = o_own_ref[z, d, :, lanes]
            heads[at, other_at, :] = o_other_ref[z, d, :, lanes]
        for k in range(HALF):
            at = n * HALF + k
            value = rows_ref[KVL : 2 * KVL, k * VD : (k + 1) * VD]
            wide[at] = lax.dot_general(
                heads[at], value, (((0,), (1,)), ((), ())), preferred_element_type=jnp.float32
            ).astype(bf16)
            send(wide.at[at, part], d_out.at[half * HALF + k])
    for copy in copies:
        copy.wait()


def rest(rows, rows_other, o_own, o_other, q_out):
    return pl.pallas_call(
        rest_kernel,
        in_specs=[VMEM] * 4 + [ANY],
        out_specs=[ANY, ANY],
        scratch_shapes=[
            pltpu.VMEM((X * HALF, F, Q_BLOCK, KVL), bf16),
            pltpu.VMEM((HEADS, VD, 512), bf16),
            pltpu.VMEM((HEADS, 512, KVL), bf16),
            pltpu.SemaphoreType.DMA((X * HALF + HEADS,)),
        ],
        out_shape=[
            jax.ShapeDtypeStruct((HEADS, F, X, Q_BLOCK, KVL), bf16),
            jax.ShapeDtypeStruct((HEADS, D_PART, KVL), bf16),
        ],
        input_output_aliases={4: 0},
        compiler_params=limit(20),
        cost_estimate=COST,
    )(rows, rows_other, o_own, o_other, q_out)


def on_device(q_nope, kv_up, o_proj):
    zh = lax.axis_index("zh")
    over = lambda a, *d: lax.ppermute(a, BULK, shifts(*d))
    core = (0, 0, 1)

    packed, o_send = pack(q_nope, kv_up, o_proj)
    packed = lax.all_to_all(packed, OWNERS, split_axis=0, concat_axis=0, tiled=True)
    o_x = [o_send[0]] + [over(o_send[d], d, 0, 0) for d in (1, 2, 3)]
    packed, o_x = lax.optimization_barrier((packed, o_x))

    own, part = unpack(packed.reshape(F * ZH * C * 16, 640), zh)
    same = over(part, 2, 0, 0)
    near = [over(own, 1, 0, 0), over(own, 3, 0, 0)]
    cross = over(same, 0, 1, 0)
    half = lambda z: jnp.stack(
        [lax.dynamic_slice_in_dim(o, z * (2 * D_PART), 2 * D_PART, 1) for o in o_x]
    )
    o_z = over(half(1 - zh), 0, 1, 0)
    near, same, cross, o_z = lax.optimization_barrier((near, same, cross, o_z))

    o_own = jnp.stack([half(zh), o_z])
    o_other = over(o_own, *core)
    rows = sort_rows(zh, own, *near, same, cross)
    rows_other = over(rows, *core)
    q_out = query(rows)
    q_out, d_out = rest(rows, rows_other, o_own, o_other, q_out)
    return q_out.reshape(HEADS, QL, KVL), d_out.transpose(0, 2, 1)


def solution(mesh):
    fine = Mesh(mesh.devices.reshape(ZL, Y, X, ZH, C), ("zl", "y", "x", "zh", "c"))
    rows = P(("zl", "y", "x", "zh", "c"), None)
    return jax.shard_map(
        on_device,
        mesh=fine,
        in_specs=(rows, rows, rows),
        out_specs=(P(("zl", "y"), None, None), P(("zl", "y"), None, BULK)),
        check_vma=False,
    )
```

```python
import jax
import jax.numpy as jnp
from jax import lax
from jax.experimental import pallas as pl
from jax.experimental.pallas import tpu as pltpu
from jax.sharding import Mesh, PartitionSpec as P

QL = 1536
KVL = 512
NOPE = 128
VD = 128
X, ZH, ZL, Y, C = 4, 2, 2, 4, 2
BULK = ("x", "zh", "c")
OWNERS = ("zl", "y", "zh", "c")
F = ZL * Y
HEADS = 8
HALF = 4
WIDE = HALF * NOPE
Q_ROWS, KV_ROWS = 12, 4
Q_BLOCK = ZH * C * Q_ROWS
Q_ALL = F * Q_BLOCK
L_BLOCK = ZH * C * KV_ROWS
ROWS = Q_ALL + 2 * F * L_BLOCK
D_PART = 448
bf16 = jnp.bfloat16
PACK_MIB = 56
EXTRA = 48
VMEM = pl.BlockSpec(memory_space=pltpu.VMEM)
ANY = pl.BlockSpec(memory_space=pl.ANY)


def shifts(dx, dz, dc):
    at = lambda x, z, c: (x * ZH + z) * C + c
    return [
        (at(x, z, c), at((x + dx) % X, (z + dz) % ZH, (c + dc) % C))
        for x in range(X)
        for z in range(ZH)
        for c in range(C)
    ]


COST = pl.CostEstimate(flops=1024, bytes_accessed=1024, transcendentals=0)


def limit(mib):
    return pltpu.CompilerParams(vmem_limit_bytes=mib * 2**20)


def pack_kernel(q_hbm, kv_hbm, o_hbm, out_ref, *refs):
    o_refs, (q_ref, kv_ref, sems) = refs[:X], refs[X:]
    kv_copy = pltpu.make_async_copy(kv_hbm, kv_ref, sems.at[0])
    q_copy = pltpu.make_async_copy(q_hbm, q_ref, sems.at[1])
    kv_copy.start()
    q_copy.start()
    copies = []
    o_cols = o_hbm.shape[1] // X
    for d in range(X):
        at = pl.multiple_of(lax.rem(lax.axis_index("x") + d, X) * o_cols, 128)
        copies.append(
            pltpu.make_async_copy(o_hbm.at[:, pl.ds(at, o_cols)], o_refs[d], sems.at[2 + d])
        )
        copies[d].start()
    kv_copy.wait()
    for n in range(F * C):
        for z in range(ZH):
            at = (n // C * ZH + z) * C + n % C
            out_ref[at, Q_ROWS:, :WIDE] = kv_ref[:, n * 1024 : n * 1024 + WIDE]
            for j in range(4):
                lane = n * 1024 + WIDE + j * 128
                out_ref[at, j * 4 : (j + 1) * 4, WIDE:] = kv_ref[:, lane : lane + 128]
    q_copy.wait()
    for n in range(F * C):
        for z in range(ZH):
            at = (n // C * ZH + z) * C + n % C
            out_ref[at, :Q_ROWS, :WIDE] = q_ref[:, n * WIDE : (n + 1) * WIDE]
    for copy in copies:
        copy.wait()


def pack(q, kv, o):
    o_cols = o.shape[1] // X
    out = pl.pallas_call(
        pack_kernel,
        in_specs=[ANY] * 3,
        out_specs=[VMEM] * (X + 1),
        out_shape=[jax.ShapeDtypeStruct((F * ZH * C, 16, 640), bf16)]
        + [jax.ShapeDtypeStruct((o.shape[0], o_cols), bf16)] * X,
        scratch_shapes=[
            pltpu.VMEM(q.shape, bf16),
            pltpu.VMEM(kv.shape, bf16),
            pltpu.SemaphoreType.DMA((2 + X,)),
        ],
        compiler_params=limit(PACK_MIB),
        cost_estimate=COST,
    )(q, kv, o)
    return out[0], out[1:]


def unpack_kernel(packed_ref, left_ref, right_ref, half_left_ref, half_right_ref, out, half_out):
    half_out[ROWS // 2 :] = jnp.zeros((EXTRA, WIDE), bf16)
    for g in range(2):
        packed = packed_ref[g * 256 : (g + 1) * 256]
        for left_by, right_by, ref in (
            (left_ref, right_ref, out),
            (half_left_ref, half_right_ref, half_out),
        ):
            left = jnp.dot(left_by[...], packed[:, :WIDE], preferred_element_type=jnp.float32)
            right = jnp.dot(right_by[...], packed[:, WIDE:], preferred_element_type=jnp.float32)
            left, right = left.astype(bf16), right.astype(bf16)
            rows_l = left_by.shape[0] // 4
            rows_q = 3 * rows_l
            ref[g * rows_q : (g + 1) * rows_q] = left[:rows_q]
            at = (2 * 3 + g) * rows_l
            ref[at : at + rows_l] = left[rows_q:]
            at += 2 * rows_l
            for j in range(4):
                lanes = slice(j * 128, (j + 1) * 128)
                ref[at : at + rows_l, lanes] = right[j * rows_l : (j + 1) * rows_l]


def unpack(packed, zh):
    column = jnp.arange(256)[None, :]

    def select(sources, first):
        size = sources * 16
        row = jnp.arange(4 * size)
        block = lambda n: n // sources * 4 + n % sources + first
        of_q = block(row // Q_ROWS) * 16 + row % Q_ROWS
        r = row % size
        of_kv = block(r // KV_ROWS) * 16 + r % KV_ROWS
        left = jnp.where(row < 3 * size, of_q, of_kv + Q_ROWS)
        right = of_kv + row // size * 4
        return [(source[:, None] == column).astype(bf16) for source in (left, right)]

    return pl.pallas_call(
        unpack_kernel,
        out_shape=[
            jax.ShapeDtypeStruct((ROWS, WIDE), bf16),
            jax.ShapeDtypeStruct((ROWS // 2 + EXTRA, WIDE), bf16),
        ],
        compiler_params=limit(8),
        cost_estimate=COST,
    )(packed, *select(4, 0), *select(2, zh * 2))


def sort_kernel(own, right, left, same_ref, cross_ref, by_q_ref, by_l_ref, o_ref, out, o_out, far, kv):
    there = pl.ds(pl.multiple_of((1 - lax.axis_index("c")) * 384, 128), 512)
    o_out[...] = o_ref[:, :, :, there]
    half_q, half_l = Q_ALL // 4, F * L_BLOCK // 2
    for g in range(2):
        at = slice(g * half_q, (g + 1) * half_q)
        block = jnp.concatenate([same_ref[at], cross_ref[at]], axis=0)
        block = jnp.dot(by_q_ref[...], block, preferred_element_type=jnp.float32)
        far[2 * g * half_q : 2 * (g + 1) * half_q] = block.astype(bf16)
    for h in range(2):
        at = slice(Q_ALL // 2 + h * half_l, Q_ALL // 2 + (h + 1) * half_l)
        block = jnp.concatenate([same_ref[at], cross_ref[at]], axis=0)
        block = jnp.dot(by_l_ref[...], block, preferred_element_type=jnp.float32)
        at = Q_ALL + 2 * h * half_l
        far[at : at + 2 * half_l] = block.astype(bf16)
    for d, ref in enumerate((own, right, far, left)):
        xs = lax.rem(lax.axis_index("x") - d + X, X)
        for f in range(F):
            at = pl.multiple_of(f * (X * L_BLOCK) + xs * L_BLOCK, L_BLOCK)
            for h in range(2):
                source = Q_ALL + (h * F + f) * L_BLOCK
                rows = ref[source : source + L_BLOCK]
                kv[pl.ds(at, L_BLOCK), h * WIDE : (h + 1) * WIDE] = rows
        out[2 * KVL + d * Q_ALL : 2 * KVL + (d + 1) * Q_ALL] = ref[:Q_ALL]
    for k in range(HALF):
        out[k * NOPE : (k + 1) * NOPE] = kv[:, k * 256 : k * 256 + NOPE].T
        out[KVL : 2 * KVL, k * VD : (k + 1) * VD] = kv[:, k * 256 + NOPE : (k + 1) * 256]


def interleave(blocks, size, zh):
    row = jnp.arange(2 * blocks * size)
    z = row // size % ZH
    source = jnp.where(z == zh, 0, blocks * size) + row // (ZH * size) * size + row % size
    return (source[:, None] == row[None, :]).astype(bf16)


def sort_rows(zh, own, right, left, same, cross, o_own):
    return pl.pallas_call(
        sort_kernel,
        out_shape=[
            jax.ShapeDtypeStruct((2 * KVL + X * Q_ALL, WIDE), bf16),
            jax.ShapeDtypeStruct((ZH, X, 64, 512), bf16),
        ],
        scratch_shapes=[pltpu.VMEM((ROWS, WIDE), bf16), pltpu.VMEM((KVL, 1024), bf16)],
        compiler_params=limit(12),
        cost_estimate=COST,
    )(own, right, left, same, cross, interleave(F // 2, 24, zh), interleave(F, 8, zh), o_own)


def sender(sems):
    copies = []

    def send(source, target):
        copy = pltpu.make_async_copy(source, target, sems.at[len(copies)])
        copy.start()
        copies.append(copy)

    return copies, send


def query_blocks(x, half, rows_ref, q_out, blocks, send):
    for d in range(X):
        xs = lax.rem(x - d + X, X)
        first = 2 * KVL + d * Q_ALL
        for k in range(HALF):
            lanes = slice(k * NOPE, (k + 1) * NOPE)
            block = jnp.dot(
                rows_ref[first : first + Q_ALL, lanes],
                rows_ref[lanes],
                preferred_element_type=jnp.float32,
            )
            at = d * HALF + k
            blocks[at] = block.astype(bf16).reshape(F, Q_BLOCK, KVL)
            send(blocks.at[at], q_out.at[half * HALF + k, :, xs])


def query_kernel(rows_ref, q_out, blocks, sems):
    copies, send = sender(sems)
    query_blocks(lax.axis_index("x"), lax.axis_index("c"), rows_ref, q_out, blocks, send)
    for copy in copies:
        copy.wait()


def query(rows):
    return pl.pallas_call(
        query_kernel,
        in_specs=[VMEM],
        out_specs=ANY,
        scratch_shapes=[
            pltpu.VMEM((X * HALF, F, Q_BLOCK, KVL), bf16),
            pltpu.SemaphoreType.DMA((X * HALF,)),
        ],
        out_shape=jax.ShapeDtypeStruct((HEADS, F, X, Q_BLOCK, KVL), bf16),
        compiler_params=limit(16),
        cost_estimate=COST,
    )(rows)


def rest_kernel(own_ref, other_ref, o_own_ref, o_other_ref, _, q_out, d_out, *scratch):
    blocks, heads, wide, sems = scratch
    x, zh, c = (lax.axis_index(a) for a in BULK)
    copies, send = sender(sems)
    lanes = pl.ds(pl.multiple_of(c * 384, 128), 512)
    own_at = pl.ds(pl.multiple_of(c * 64, 64), 64)
    other_at = pl.ds(pl.multiple_of((1 - c) * 64, 64), 64)
    part = pl.ds(pl.multiple_of(c * 64, 64), D_PART)
    query_blocks(x, 1 - c, other_ref, q_out, blocks, send)
    for n, (rows_ref, half) in enumerate(((own_ref, c), (other_ref, 1 - c))):
        for k in range(HALF):
            d = lax.rem(x - (2 * half + k // 2) + X, X)
            z = lax.rem(zh + k, 2)
            at = n * HALF + k
            heads[at, own_at, :] = o_own_ref[z, d, :, lanes]
            heads[at, other_at, :] = o_other_ref[z, d]
        for k in range(HALF):
            at = n * HALF + k
            value = rows_ref[KVL : 2 * KVL, k * VD : (k + 1) * VD]
            wide[at] = lax.dot_general(
                heads[at], value, (((0,), (1,)), ((), ())), preferred_element_type=jnp.float32
            ).astype(bf16)
            send(wide.at[at, part], d_out.at[half * HALF + k])
    for copy in copies:
        copy.wait()


def rest(rows, rows_other, o_own, o_other, q_out):
    return pl.pallas_call(
        rest_kernel,
        in_specs=[VMEM] * 4 + [ANY],
        out_specs=[ANY, ANY],
        scratch_shapes=[
            pltpu.VMEM((X * HALF, F, Q_BLOCK, KVL), bf16),
            pltpu.VMEM((HEADS, VD, 512), bf16),
            pltpu.VMEM((HEADS, 512, KVL), bf16),
            pltpu.SemaphoreType.DMA((X * HALF + HEADS,)),
        ],
        out_shape=[
            jax.ShapeDtypeStruct((HEADS, F, X, Q_BLOCK, KVL), bf16),
            jax.ShapeDtypeStruct((HEADS, D_PART, KVL), bf16),
        ],
        input_output_aliases={4: 0},
        compiler_params=limit(20),
        cost_estimate=COST,
    )(rows, rows_other, o_own, o_other, q_out)


def on_device(q_nope, kv_up, o_proj):
    zh = lax.axis_index("zh")
    over = lambda a, *d: lax.ppermute(a, BULK, shifts(*d))
    core = (0, 0, 1)

    packed, o_send = pack(q_nope, kv_up, o_proj)
    packed = lax.all_to_all(packed, OWNERS, split_axis=0, concat_axis=0, tiled=True)
    o_x = [o_send[0]] + [over(o_send[d], d, 0, 0) for d in (1, 2, 3)]
    packed, o_x = lax.optimization_barrier((packed, o_x))

    own, part = unpack(packed.reshape(F * ZH * C * 16, 640), zh)
    same = over(part, 2, 0, 0)
    near = [over(own, 1, 0, 0), over(own, 3, 0, 0)]
    cross = over(same, 0, 1, 0)
    half = lambda z: jnp.stack(
        [lax.dynamic_slice_in_dim(o, z * (2 * D_PART), 2 * D_PART, 1) for o in o_x]
    )
    o_z = over(half(1 - zh), 0, 1, 0)
    near, same, cross, o_z = lax.optimization_barrier((near, same, cross, o_z))

    o_own = jnp.stack([half(zh), o_z])
    rows, o_window = sort_rows(zh, own, *near, same, cross, o_own)
    o_other = over(o_window, *core)
    rows_other = over(rows, *core)
    q_out = query(rows)
    q_out, d_out = rest(rows, rows_other, o_own, o_other, q_out)
    return q_out.reshape(HEADS, QL, KVL), d_out.transpose(0, 2, 1)


def solution(mesh):
    fine = Mesh(mesh.devices.reshape(ZL, Y, X, ZH, C), ("zl", "y", "x", "zh", "c"))
    rows = P(("zl", "y", "x", "zh", "c"), None)
    return jax.shard_map(
        on_device,
        mesh=fine,
        in_specs=(rows, rows, rows),
        out_specs=(P(("zl", "y"), None, None), P(("zl", "y"), None, BULK)),
        check_vma=False,
    )
```
